256 devices in a mesh: tm: 4 (over y_hi, core), shot: 64 (over x, y_lo, z).
Axes of the slice: x: 4, y: 4 (y_hi: 2, y_lo: 2; y = y_hi * 2 + y_lo), z: 8, core: 2. Of those that a mesh axis runs over, the one named last changes fastest.
Arguments:
- traces: bfloat16 [2048, 128, 4096], P('shot', None, 'tm'), may hold values from -6 to 6
- shot_pos: int32 [2048], P('shot'), may hold values from 0 to 4095
- slowness: int32 [128], replicated, may hold values from -64 to 64
Outputs:
- records: float32 [256, 2, 128, 128], P(('tm', 'shot'))
The draws below stay inside these ranges and needn't reach their ends.
All inputs are finite; a program needn't handle non-finite values.
Results may differ from the reference program's by a relative error of at most 0.0023.
Values sent between devices are 32-bit elements; how exact they have to be, the bound alone decides.
No kernel may reach another device: no remote copies, remote signals or barrier semaphores. Data moves between devices by JAX's collectives and lax.ppermute only.
A program may use at most 128 MiB of HBM per device.

```python
import math
import jax
import jax.numpy as jnp
from jax import lax

NT = 4096
REC = 128
F = 256
P_SIZE = 128
FREQ0 = 16
S_DEV = 32
SHOTS = 2048
N_SHOT = 64


def set_ends(array, own_key, smallest, top_value):
    longest = array.shape.index(max(array.shape))
    spots = []
    for shift in (0, 1):
        where = [jax.random.randint(jax.random.fold_in(own_key, axis), (), 0, length) for axis, length in enumerate(array.shape)]
        where[longest] = (where[longest] + shift) % array.shape[longest]
        spots.append(tuple(where))
    return array.at[spots[0]].set(smallest).at[spots[1]].set(top_value)


def level_of(rng, shape, cuts, least, top_value):
    gain = 1.0
    for axis_at, blocks in cuts:
        heights = jax.random.uniform(jax.random.fold_in(jax.random.fold_in(rng, 6), axis_at), (blocks,), jnp.float32, least / len(cuts), top_value / len(cuts))
        gain = gain * jnp.repeat(jnp.exp(heights), shape[axis_at] // blocks).reshape((-1,) + (1,) * (len(shape) - 1 - axis_at))
    return gain


def noise(rng, extent, width, bound, cuts=(), kind=jnp.bfloat16):
    level = level_of(rng, extent, cuts, -0.22, 0.18) if cuts else 1.0
    array = jax.random.normal(rng, extent, jnp.float32) * width * level
    return jnp.minimum(jnp.maximum(array, -bound), bound).astype(kind)


def setup_inputs(seed: int = 0) -> dict:
    seeds = jax.random.split(jax.random.key(seed), 4)
    return {
        "traces": noise(seeds[0], (SHOTS, REC, NT), 1.0, 6.0, ((0, 64), (2, 4))),
        "shot_pos": set_ends(jax.random.randint(seeds[1], (SHOTS,), 0, NT), jax.random.fold_in(seeds[1], 1), 0, NT - 1).astype(jnp.int32),
        "slowness": set_ends(jax.random.randint(seeds[2], (P_SIZE,), -64, 65), jax.random.fold_in(seeds[2], 1), -64, 64).astype(jnp.int32),
    }


def reference(traces, shot_pos, slowness):
    times = jnp.arange(NT, dtype=jnp.int32)
    freq_bins = FREQ0 + jnp.arange(F, dtype=jnp.int32)
    phase_index = times[:, None] * freq_bins[None, :] % NT
    angle = phase_index.astype(jnp.float32) * (2.0 * math.pi / NT)
    cosine = jnp.cos(angle).astype(jnp.bfloat16).astype(jnp.float32)
    sine_part = (-jnp.sin(angle)).astype(jnp.bfloat16).astype(jnp.float32)
    table = jnp.concatenate([cosine, sine_part], axis=1)

    def shot_block(block):
        flat = block.reshape(-1, NT).astype(jnp.float32)
        return jnp.dot(flat, table, preferred_element_type=jnp.float32)
    blocks = traces.reshape(N_SHOT, S_DEV, REC, NT)
    spectra = lax.map(shot_block, blocks)
    spectrum = spectra.reshape(SHOTS, REC, 2, F) * jnp.float32(1.0 / math.sqrt(NT))
    spectrum = jnp.transpose(spectrum, (3, 2, 0, 1))
    delay_index = slowness[:, None] * shot_pos[None, :] % NT
    shot_scale = jnp.float32(1.0 / math.sqrt(SHOTS))

    def per_freq(inputs):
        spec, freq_bin = inputs
        phase = (freq_bin * delay_index % NT).astype(jnp.float32) * (2.0 * math.pi / NT)
        phase_cosine = jnp.cos(phase)
        phase_sine = jnp.sin(phase)
        highest_precision = lax.Precision.HIGHEST
        receiver_real = jnp.dot(phase_cosine, spec[0], precision=highest_precision) + jnp.dot(phase_sine, spec[1], precision=highest_precision)
        receiver_imaginary = jnp.dot(phase_cosine, spec[1], precision=highest_precision) - jnp.dot(phase_sine, spec[0], precision=highest_precision)
        return jnp.stack([receiver_real, receiver_imaginary], axis=0) * shot_scale
    return lax.map(per_freq, (spectrum, freq_bins))
```

```python
import math

import jax
import jax.numpy as jnp
import numpy as np
from jax import lax
from jax.experimental import pallas as pl
from jax.experimental.pallas import tpu as pltpu
from jax.sharding import Mesh, PartitionSpec as P

NT = 4096
REC = 128
F = 256
NP = 128
FREQ0 = 16
S_DEV = 32
T_DEV = 1024
SHOTS = 2048
FINE = ("yh", "c", "x", "yl", "zh", "zl")
SIZES = (2, 2, 4, 2, 4, 2)
GROUP = ("yh", "x", "yl", "zl")
N_GROUP = 32
N_SRC = 16
N_ZH = 4
VMEM = 60 * 1024 * 1024


def dft_tables():
    yh, x, yl, zl, zh = np.meshgrid(*(np.arange(n) for n in (2, 4, 2, 2, 4)), indexing="ij")
    base = (yh * 128 + x * 16 + yl * 8 + zh * 2 + zl).reshape(-1)
    out = np.empty((2, 2, 2, 128, 2, T_DEV), np.float64)
    for y in range(2):
        for c in range(2):
            t = (y * 2 + c) * T_DEV + np.arange(T_DEV)
            for half in range(2):
                k = FREQ0 + base + 64 * (c ^ half)
                angle = (k[:, None] * t[None, :] % NT) * (2.0 * math.pi / NT)
                out[y, c, half, :, 0] = np.cos(angle)
                out[y, c, half, :, 1] = -np.sin(angle)
    return out.reshape(4, 2, 256, T_DEV).astype(np.float32).astype(jnp.bfloat16)


def dft_body(table, traces, out):
    block = traces[...]
    rows = block.shape[0]
    res = lax.dot_general(
        table[...], block.reshape(rows * REC, T_DEV), (((1,), (1,)), ((), ())), preferred_element_type=jnp.float32
    )
    for s in range(rows):
        out[:, s] = res[:, s * REC : (s + 1) * REC].reshape(N_GROUP, 8, REC)


def dft_add_body(table, traces, other, out):
    block = traces[...]
    rows = block.shape[0]
    res = lax.dot_general(
        table[...], block.reshape(rows * REC, T_DEV), (((1,), (1,)), ((), ())), preferred_element_type=jnp.float32
    )
    for s in range(rows):
        out[:, s] = res[:, s * REC : (s + 1) * REC].reshape(N_GROUP, 8, REC) + other[:, s]


def dft(table, traces, other=None):
    step = 4
    spec = pl.BlockSpec((N_GROUP, step, 8, REC), lambda i: (0, i, 0, 0))
    in_specs = [
        pl.BlockSpec((256, T_DEV), lambda i: (0, 0)),
        pl.BlockSpec((step, REC, T_DEV), lambda i: (i, 0, 0)),
    ]
    args = [table, traces]
    if other is not None:
        in_specs.append(spec)
        args.append(other)
    return pl.pallas_call(
        dft_body if other is None else dft_add_body,
        grid=(S_DEV // step,),
        in_specs=in_specs,
        out_specs=spec,
        out_shape=jax.ShapeDtypeStruct((N_GROUP, S_DEV, 8, REC), jnp.float32),
        compiler_params=pltpu.CompilerParams(vmem_limit_bytes=VMEM),
        cost_estimate=pl.CostEstimate(flops=2 * 256 * 4096 * 1024, bytes_accessed=12 << 20, transcendentals=0),
        name="dft",
    )(*args)


def split(value):
    high = value.astype(jnp.bfloat16)
    return high, (value - high.astype(jnp.float32)).astype(jnp.bfloat16)


def phase_body(first, slowness, positions, high, low):
    delay = (slowness[...] * positions[...]) & (NT - 1)
    for j in range(N_ZH):
        index = ((first[0] + 2 * j) * delay) & (NT - 1)
        quadrant = (index + NT // 8) >> 10
        u = (index - (quadrant << 10)).astype(jnp.float32) * (2.0 * math.pi / NT)
        v = u * u
        sine = u + u * v * (-1.0 / 6 + v * (1.0 / 120 + v * (-1.0 / 5040 + v * (1.0 / 362880))))
        cosine = 1.0 + v * (-0.5 + v * (1.0 / 24 + v * (-1.0 / 720 + v * (1.0 / 40320 + v * (-1.0 / 3628800)))))
        odd = (quadrant & 1) == 1
        c = jnp.where(odd, sine, cosine)
        s = jnp.where(odd, cosine, sine)
        c = jnp.where(((quadrant + 1) & 2) == 2, -c, c)
        s = jnp.where((quadrant & 2) == 2, -s, s)
        high[j, :NP], low[j, :NP] = split(c)
        high[j, NP:], low[j, NP:] = split(s)


def phase_tables(first, slowness, positions):
    shape = jax.ShapeDtypeStruct((N_ZH, 2 * NP, N_SRC * S_DEV), jnp.bfloat16)
    return pl.pallas_call(
        phase_body,
        in_specs=[
            pl.BlockSpec(memory_space=pltpu.SMEM),
            pl.BlockSpec(memory_space=pltpu.VMEM),
            pl.BlockSpec(memory_space=pltpu.VMEM),
        ],
        out_specs=[pl.BlockSpec(memory_space=pltpu.VMEM)] * 2,
        out_shape=[shape, shape],
        compiler_params=pltpu.CompilerParams(vmem_limit_bytes=VMEM),
        name="phase_tables",
    )(first, slowness.reshape(NP, 1), positions.reshape(1, N_SRC * S_DEV))


def slant_body(high, low, spectra, out):
    shots = N_SRC * S_DEV
    for j in range(N_ZH):
        cols = []
        for part in range(2):
            where = pl.ds(2 * j + part, shots, stride=8)
            cols.append(spectra[0, where, :] + spectra[1, where, :])
        b_high, b_low = split(jnp.concatenate(cols, axis=1))
        a = high[j]
        dot = lambda m, n: jnp.dot(m, n, preferred_element_type=jnp.float32)
        res = dot(a, b_high) + (dot(low[j], b_high) + dot(a, b_low))
        out[j, 0] = res[:NP, :REC] + res[NP:, REC:]
        out[j, 1] = res[:NP, REC:] - res[NP:, :REC]


def slant(high, low, spectra):
    return pl.pallas_call(
        slant_body,
        in_specs=[pl.BlockSpec(memory_space=pltpu.VMEM)] * 3,
        out_specs=pl.BlockSpec(memory_space=pltpu.VMEM),
        out_shape=jax.ShapeDtypeStruct((N_ZH, 2, NP, REC), jnp.float32),
        compiler_params=pltpu.CompilerParams(vmem_limit_bytes=VMEM),
        name="slant",
    )(high, low, spectra.reshape(2, N_SRC * S_DEV * 8, REC))


def body(traces, shot_pos, slowness):
    index = {name: lax.axis_index(name) for name in FINE}
    tables = lax.dynamic_index_in_dim(jnp.asarray(dft_tables()), index["yh"] * 2 + index["c"], 0, keepdims=False)
    positions = lax.all_gather(shot_pos, ("x", "yl", "zl"), tiled=True)
    first = FREQ0 + index["yh"] * 128 + index["c"] * 64 + index["x"] * 16 + index["yl"] * 8 + index["zl"]
    high, low = phase_tables(first.reshape(1).astype(jnp.int32), slowness, positions)

    other = dft(tables[1], traces)
    other = lax.ppermute(other, "c", [(0, 1), (1, 0)])
    mine = dft(tables[0], traces, other)
    spectra = lax.all_to_all(mine, GROUP, 0, 0, tiled=True)
    partial = slant(high, low, spectra)
    partial = lax.all_to_all(partial, "zh", 0, 0, tiled=True)
    scale = jnp.float32(1.0 / math.sqrt(NT) / math.sqrt(SHOTS))
    return jnp.sum(partial, axis=0, keepdims=True) * scale


def solution(mesh):
    fine = Mesh(mesh.devices.reshape(SIZES), FINE)
    shot, tm = ("x", "yl", "zh", "zl"), ("yh", "c")
    return jax.shard_map(
        body,
        mesh=fine,
        in_specs=(P(shot, None, tm), P(shot), P()),
        out_specs=P(tm + shot, None, None, None),
        check_vma=False,
    )
```

```python
import functools
import math

import jax
import jax.numpy as jnp
import numpy as np
from jax import lax
from jax.experimental import pallas as pl
from jax.experimental.pallas import tpu as pltpu
from jax.sharding import Mesh, PartitionSpec as P

NT = 4096
REC = 128
NP = 128
FREQ0 = 16
S_DEV = 32
T_DEV = 1024
SHOTS = 2048
HALF = REC // 2
PAIRS = S_DEV // 2
FINE = ("yh", "c", "x", "yl", "zh", "zl")
SIZES = (2, 2, 4, 2, 4, 2)
N_Y = 4
N_XZ = 8
N_ZH = 4
MIB = 1024 * 1024
WHOLE = pl.BlockSpec(memory_space=pltpu.VMEM)
SCALAR = pl.BlockSpec(memory_space=pltpu.SMEM)
ANY = pl.BlockSpec(memory_space=pl.ANY)


def params(flops, size, vmem=24):
    return dict(
        compiler_params=pltpu.CompilerParams(vmem_limit_bytes=vmem * MIB),
        cost_estimate=pl.CostEstimate(flops=flops, bytes_accessed=size, transcendentals=0),
    )


def dft_tables():
    d, x, zl, zh = np.meshgrid(*(np.arange(n) for n in (N_Y, 4, 2, N_ZH)), indexing="ij")
    out = np.empty((2, 2, 2, 2, 128, 2, T_DEV), np.float64)
    for yh, c, yl, half in np.ndindex(2, 2, 2, 2):
        t = (yh * 2 + c) * T_DEV + np.arange(T_DEV)
        f = (yh ^ (d >> 1)) * 128 + (c ^ half) * 64 + x * 16 + (yl ^ (d & 1)) * 8 + zh * 2 + zl
        angle = ((FREQ0 + f).reshape(-1, 1) * t % NT) * (2.0 * math.pi / NT)
        out[yh, c, yl, half, :, 0] = np.cos(angle)
        out[yh, c, yl, half, :, 1] = -np.sin(angle)
    return out.reshape(8, 2, 256, T_DEV).astype(np.float32).astype(jnp.bfloat16)


def spectra(table, traces):
    rows = traces.shape[0]
    res = lax.dot_general(
        table[0, 0], traces[...].reshape(rows * HALF, T_DEV), (((1,), (1,)), ((), ())), preferred_element_type=jnp.float32
    )
    return [res[:, s * 128 : (s + 1) * 128].reshape(N_Y, N_XZ, 8, 128) for s in range(rows // 2)]


def other_body(n_after, index, table, traces, *rest):
    out = rest[n_after]
    for s, block in enumerate(spectra(table, traces)):
        out[:, :, s] = block


def mine_a_body(n_after, index, table, traces, other, *rest):
    outs = rest[n_after:]
    for s, block in enumerate(spectra(table, traces)):
        for d, out in enumerate(outs):
            out[:, s] = block[d] + other[d, :, s]


def mine_b_body(n_after, index, table, traces, other, here, there, *rest):
    out = rest[n_after]
    step = pl.program_id(0)
    blocks = spectra(table, traces)
    for s, block in enumerate(blocks):
        for d in range(N_Y):
            out[:, d * PAIRS + step * len(blocks) + s] = block[d] + other[d, :, s]

    @pl.when(step == 0)
    def _():
        tile = jnp.concatenate([here[:2], there[:2], jnp.zeros((4, 128), jnp.float32)], axis=0)
        out[:, N_Y * PAIRS] = jnp.broadcast_to(tile, (N_XZ, 8, 128))


def dft(index, tables, traces, half, chunk, other=None, after=(), places=()):
    step = 16
    n = step // 2
    by_d = pl.BlockSpec((N_Y, N_XZ, n, 8, 128), lambda i, index: (0, 0, i, 0, 0))
    f32 = lambda *shape: jax.ShapeDtypeStruct(shape, jnp.float32)
    if other is None:
        body, out_specs, out_shape = other_body, by_d, f32(N_Y, N_XZ, PAIRS, 8, 128)
    elif chunk == 0:
        body = mine_a_body
        out_specs = [pl.BlockSpec((N_XZ, n, 8, 128), lambda i, index: (0, i, 0, 0))] * N_Y
        out_shape = [f32(N_XZ, PAIRS, 8, 128)] * N_Y
    else:
        body = mine_b_body
        out_specs = pl.BlockSpec((N_XZ, N_Y * PAIRS + 1, 8, 128), lambda i, index: (0, 0, 0, 0))
        out_shape = f32(N_XZ, N_Y * PAIRS + 1, 8, 128)
    return pl.pallas_call(
        functools.partial(body, len(after)),
        grid_spec=pltpu.PrefetchScalarGridSpec(
            num_scalar_prefetch=1,
            grid=(S_DEV // step,),
            in_specs=[
                pl.BlockSpec((1, 1, 256, T_DEV), lambda i, index: (index[0], half, 0, 0)),
                pl.BlockSpec((step, HALF, T_DEV), lambda i, index: (i, chunk, 0)),
            ]
            + ([] if other is None else [by_d])
            + [pl.BlockSpec((8, 128), lambda i, index: (0, 0))] * len(places)
            + [ANY] * len(after),
            out_specs=out_specs,
        ),
        out_shape=out_shape,
        name=("other" if other is None else "mine") + ("_a", "_b")[chunk],
        **params(2 * 256 * 2048 * 1024, 7 << 20, 50),
    )(index, tables, traces, *([] if other is None else [other]), *places, *after)


def sum_a_body(own, yl, yh, both, *rest):
    out = rest[-1]
    out[:, 0] = own[...] + yh[...]
    out[:, 1] = yl[...] + both[...]


def sum_a(parts, after=()):
    spec = pl.BlockSpec((2, PAIRS, 8, 128), lambda i: (i, 0, 0, 0))
    return pl.pallas_call(
        sum_a_body,
        grid=(N_XZ // 2,),
        in_specs=[spec] * N_Y + [ANY] * len(after),
        out_specs=pl.BlockSpec((2, 2, PAIRS, 8, 128), lambda i: (i, 0, 0, 0, 0)),
        out_shape=jax.ShapeDtypeStruct((N_XZ, 2, PAIRS, 8, 128), jnp.float32),
        name="sum_a",
        **params(1 << 18, 3 << 20),
    )(*parts, *after)


def split(value):
    high = value.astype(jnp.bfloat16)
    return high, (value - high.astype(jnp.float32)).astype(jnp.bfloat16)


def turn(index):
    index = index & (NT - 1)
    quadrant = (index + NT // 8) >> 10
    u = (index - (quadrant << 10)).astype(jnp.float32) * (2.0 * math.pi / NT)
    v = u * u
    sine = u + u * v * (-1.0 / 6 + v * (1.0 / 120 + v * (-1.0 / 5040 + v * (1.0 / 362880))))
    cosine = 1.0 + v * (-0.5 + v * (1.0 / 24 + v * (-1.0 / 720 + v * (1.0 / 40320 + v * (-1.0 / 3628800)))))
    odd = (quadrant & 1) == 1
    c = jnp.where(odd, sine, cosine)
    s = jnp.where(odd, cosine, sine)
    return jnp.where(((quadrant + 1) & 2) == 2, -c, c), jnp.where((quadrant & 2) == 2, -s, s)


def times(a, b):
    return a[0] * b[0] - a[1] * b[1], a[1] * b[0] + a[0] * b[1]


def phase_tables(n_d, base, yh, yl, slowness, positions, column, slow, high, low):
    slow[...] = jnp.broadcast_to(slowness[...].astype(jnp.float32), (NP, 128)).T.astype(jnp.int32)
    first = base[0] + yh[0] * 128 + yl[0] * 8
    rows = 16

    def step(i, _):
        row = pl.multiple_of(i * rows, rows)
        delay = (slow[pl.ds(row, rows), :] * positions) & (NT - 1)
        own = turn(first * delay)
        forms = [own]
        if n_d > 1:
            by_yl = turn((8 - 16 * yl[0]) * delay)
            by_yh = turn((128 - 256 * yh[0]) * delay)
            other = times(own, by_yh)
            forms = [own, times(own, by_yl), other, times(other, by_yl)]
        by_zh = turn(2 * delay)
        for d, value in enumerate(forms):
            for j in range(N_ZH):
                if j > 0:
                    value = times(value, by_zh)
                for k in range(2):
                    where = (d * N_ZH + j, pl.ds(k * NP + row, rows), slice(column, column + 128))
                    high[where], low[where] = split(value[k])
        return 0

    lax.fori_loop(0, NP // rows, step, 0)


def stack(high, low, real, imag):
    left = lax.broadcasted_iota(jnp.int32, real.shape, 1) < HALF
    even = jnp.where(left, real, pltpu.roll(imag, HALF, 1))
    odd = jnp.where(left, pltpu.roll(real, HALF, 1), imag)
    b_high, b_low = split(jnp.concatenate([even, odd], axis=0))
    both = jnp.dot(high, jnp.concatenate([b_high, b_low], axis=1), preferred_element_type=jnp.float32)
    res = both[:, :128] + (jnp.dot(low, b_high, preferred_element_type=jnp.float32) + both[:, 128:])
    cross = pltpu.roll(res[NP:], HALF, 1)
    left = lax.broadcasted_iota(jnp.int32, (NP, 128), 1) < HALF
    return res[:NP] + jnp.where(left, cross, -cross)


def slant_a_body(zh, base, yh, yl, slowness, places, data, *rest):
    parts, outs, (slow, high, low) = rest[:N_Y], rest[N_Y : N_Y + N_ZH], rest[N_Y + N_ZH :]
    for parity in range(2):
        for place in range(2):
            row = 2 * place + parity
            positions = places[row : row + 1, :].astype(jnp.int32)
            phase_tables(1, base, yh, yl, slowness, positions, (2 * parity + place) * 128, slow, high, low)
    for e, out in enumerate(outs):
        j = (zh[0] + e) & (N_ZH - 1)
        cols = []
        for part in range(2):
            rows = [data[:, pl.ds(place * PAIRS * 8 + 2 * j + part, PAIRS, stride=8), :] for place in range(2)]
            cols.append(jnp.concatenate([row.reshape(N_XZ * PAIRS, 128) for row in rows], axis=0))
        out[0] = stack(high[j], low[j], *cols)
        out[1] = (parts[0][j] + parts[1][j]) + (parts[2][j] + parts[3][j])


def slant_a(zh, base, yh, yl, slowness, places, data, parts):
    return pl.pallas_call(
        slant_a_body,
        in_specs=[SCALAR] * 4 + [WHOLE] * (3 + N_Y),
        out_specs=[WHOLE] * N_ZH,
        out_shape=[jax.ShapeDtypeStruct((2, NP, 128), jnp.float32)] * N_ZH,
        scratch_shapes=[pltpu.VMEM((NP, 128), jnp.int32)] + [pltpu.VMEM((N_ZH, 2 * NP, 512), jnp.bfloat16)] * 2,
        name="slant_a",
        **params(1 << 30, 5 << 20),
    )(zh, base, yh, yl, slowness, places, data.reshape(N_XZ, 2 * PAIRS * 8, 128), *parts)


def slant_b_body(n_after, base, yh, yl, slowness, data, *rest):
    rest = rest[n_after:]
    outs, here, (slow, high, low) = rest[:N_Y], rest[N_Y], rest[N_Y + 1 :]
    here[...] = jnp.sum(data[:, N_Y * PAIRS * 8 :, :], axis=0)
    for parity in range(2):
        row = here[parity : parity + 1, :].astype(jnp.int32)
        phase_tables(N_Y, base, yh, yl, slowness, row, parity * 128, slow, high, low)
    for d, out in enumerate(outs):
        for j in range(N_ZH):
            cols = [
                data[:, pl.ds(d * PAIRS * 8 + 2 * j + part, PAIRS, stride=8), :].reshape(N_XZ * PAIRS, 128)
                for part in range(2)
            ]
            out[j] = stack(high[d * N_ZH + j], low[d * N_ZH + j], *cols)


def slant_b(base, yh, yl, slowness, data, after=()):
    return pl.pallas_call(
        functools.partial(slant_b_body, len(after)),
        in_specs=[SCALAR] * 3 + [WHOLE] * 2 + [ANY] * len(after),
        out_specs=[WHOLE] * (N_Y + 1),
        out_shape=[jax.ShapeDtypeStruct((N_ZH, NP, 128), jnp.float32)] * N_Y + [jax.ShapeDtypeStruct((8, 128), jnp.float32)],
        scratch_shapes=[pltpu.VMEM((NP, 128), jnp.int32)] + [pltpu.VMEM((N_Y * N_ZH, 2 * NP, 256), jnp.bfloat16)] * 2,
        name="slant_b",
        **params(1 << 31, 7 << 20),
    )(base, yh, yl, slowness, data.reshape(N_XZ, (N_Y * PAIRS + 1) * 8, 128), *after)


def finish_body(own, *rest):
    scale = jnp.float32(1.0 / math.sqrt(NT) / math.sqrt(SHOTS))
    left = lax.broadcasted_iota(jnp.int32, (NP, 128), 1) < HALF
    out = rest[-1]
    a, b = (((own[i] + rest[0][i]) + (rest[1][i] + rest[2][i])) * scale for i in range(2))
    out[0, 0] = jnp.where(left, a, pltpu.roll(b, HALF, 1))
    out[0, 1] = jnp.where(left, pltpu.roll(a, HALF, 1), b)


def finish(parts):
    return pl.pallas_call(
        finish_body,
        in_specs=[WHOLE] * N_ZH,
        out_specs=WHOLE,
        out_shape=jax.ShapeDtypeStruct((1, 2, NP, REC), jnp.float32),
        name="finish",
        **params(1 << 18, 1 << 20),
    )(*parts)


def swap(value, axes, size, mask):
    return lax.ppermute(value, axes, [(i, i ^ mask) for i in range(size)])


def exchange_y(parts):
    return [parts[0]] + [swap(parts[d], ("yh", "yl"), N_Y, d) for d in range(1, N_Y)]


def exchange_z(parts):
    shift = lambda e: [(i, (i + e) % N_ZH) for i in range(N_ZH)]
    return [parts[0]] + [lax.ppermute(parts[e], "zh", shift(e)) for e in range(1, N_ZH)]


def body(traces, shot_pos, slowness):
    yh, c, x, yl, zh, zl = (lax.axis_index(name) for name in FINE)
    one = lambda value: value.reshape(1)

    slot = (jnp.arange(N_XZ) == x * 2 + zl).astype(jnp.int32)
    places = (shot_pos.reshape(1, PAIRS, 2) * slot[:, None, None]).reshape(N_XZ * PAIRS, 2).T
    places = jnp.pad(places.astype(jnp.float32), ((0, 6), (0, 0)))

    tables = jnp.asarray(dft_tables())
    index = one(yh * 4 + c * 2 + yl)
    other_a = dft(index, tables, traces, 1, 0)
    other_b = dft(index, tables, traces, 1, 1, after=[other_a])
    mine_a = dft(index, tables, traces, 0, 0, swap(other_a, "c", 2, 1), after=[other_b])
    there = swap(places, "yl", 2, 1)
    mine_b = dft(index, tables, traces, 0, 1, swap(other_b, "c", 2, 1), after=[mine_a[0]], places=[places, there])
    data_b = lax.all_to_all(mine_b, ("x", "zl"), 0, 0, tiled=True)

    where = one(FREQ0 + c * 64 + x * 16 + zl), one(yh), one(yl), slowness.reshape(1, NP)
    *part_b, places = slant_b(*where, data_b)
    data_a = lax.all_to_all(sum_a(exchange_y(mine_a), after=[places]), ("x", "zl"), 0, 0, tiled=True)
    return finish(exchange_z(slant_a(one(zh), *where, places, data_a, exchange_y(part_b))))


def solution(mesh):
    fine = Mesh(mesh.devices.reshape(SIZES), FINE)
    shot, tm = ("x", "yl", "zh", "zl"), ("yh", "c")
    return jax.shard_map(
        body,
        mesh=fine,
        in_specs=(P(shot, None, tm), P(shot), P()),
        out_specs=P(tm + shot, None, None, None),
        check_vma=False,
    )
```

```python
import functools
import math

import jax
import jax.numpy as jnp
import numpy as np
from jax import lax
from jax.experimental import pallas as pl
from jax.experimental.pallas import tpu as pltpu
from jax.sharding import Mesh, PartitionSpec as P

NT = 4096
REC = 128
NP = 128
FREQ0 = 16
S_DEV = 32
T_DEV = 1024
SHOTS = 2048
HALF = REC // 2
PAIRS = S_DEV // 2
FINE = ("yh", "c", "x", "yl", "zh", "zl")
SIZES = (2, 2, 4, 2, 4, 2)
N_Y = 4
N_XZ = 8
N_ZH = 4
MIB = 1024 * 1024
WHOLE = pl.BlockSpec(memory_space=pltpu.VMEM)
SCALAR = pl.BlockSpec(memory_space=pltpu.SMEM)
ANY = pl.BlockSpec(memory_space=pl.ANY)


def params(flops, size, vmem=24):
    return dict(
        compiler_params=pltpu.CompilerParams(vmem_limit_bytes=vmem * MIB),
        cost_estimate=pl.CostEstimate(flops=flops, bytes_accessed=size, transcendentals=0),
    )


def dft_tables():
    d, x, zl, zh = np.meshgrid(*(np.arange(n) for n in (N_Y, 4, 2, N_ZH)), indexing="ij")
    out = np.empty((2, 2, 2, 2, 128, 2, T_DEV), np.float64)
    for yh, c, yl, half in np.ndindex(2, 2, 2, 2):
        t = (yh * 2 + c) * T_DEV + np.arange(T_DEV)
        f = (yh ^ (d >> 1)) * 128 + (c ^ half) * 64 + x * 16 + (yl ^ (d & 1)) * 8 + zh * 2 + zl
        angle = ((FREQ0 + f).reshape(-1, 1) * t % NT) * (2.0 * math.pi / NT)
        out[yh, c, yl, half, :, 0] = np.cos(angle)
        out[yh, c, yl, half, :, 1] = -np.sin(angle)
    return out.reshape(8, 2, 256, T_DEV).astype(np.float32).astype(jnp.bfloat16)


def spectra(table, traces):
    rows = traces.shape[0]
    res = lax.dot_general(
        table[0, 0], traces[...].reshape(rows * HALF, T_DEV), (((1,), (1,)), ((), ())), preferred_element_type=jnp.float32
    )
    return [res[:, s * 128 : (s + 1) * 128].reshape(N_Y, N_XZ, 8, 128) for s in range(rows // 2)]


def other_body(n_after, index, table, traces, *rest):
    out = rest[n_after]
    for s, block in enumerate(spectra(table, traces)):
        out[:, :, s] = block


def mine_a_body(n_after, index, table, traces, other, *rest):
    outs = rest[n_after:]
    for s, block in enumerate(spectra(table, traces)):
        for d, out in enumerate(outs):
            out[:, s] = block[d] + other[d, :, s]


def mine_b_body(n_after, index, table, traces, other, here, there, *rest):
    out = rest[n_after]
    step = pl.program_id(0)
    blocks = spectra(table, traces)
    for s, block in enumerate(blocks):
        for d in range(N_Y):
            out[:, d * PAIRS + step * len(blocks) + s] = block[d] + other[d, :, s]

    @pl.when(step == 0)
    def _():
        tile = jnp.concatenate([here[:2], there[:2], jnp.zeros((4, 128), jnp.float32)], axis=0)
        out[:, N_Y * PAIRS] = jnp.broadcast_to(tile, (N_XZ, 8, 128))


def dft(index, tables, traces, half, chunk, other=None, after=(), places=()):
    step = 16
    n = step // 2
    by_d = pl.BlockSpec((N_Y, N_XZ, n, 8, 128), lambda i, index: (0, 0, i, 0, 0))
    f32 = lambda *shape: jax.ShapeDtypeStruct(shape, jnp.float32)
    if other is None:
        body, out_specs, out_shape = other_body, by_d, f32(N_Y, N_XZ, PAIRS, 8, 128)
    elif chunk == 0:
        body = mine_a_body
        out_specs = [pl.BlockSpec((N_XZ, n, 8, 128), lambda i, index: (0, i, 0, 0))] * N_Y
        out_shape = [f32(N_XZ, PAIRS, 8, 128)] * N_Y
    else:
        body = mine_b_body
        out_specs = pl.BlockSpec((N_XZ, N_Y * PAIRS + 1, 8, 128), lambda i, index: (0, 0, 0, 0))
        out_shape = f32(N_XZ, N_Y * PAIRS + 1, 8, 128)
    return pl.pallas_call(
        functools.partial(body, len(after)),
        grid_spec=pltpu.PrefetchScalarGridSpec(
            num_scalar_prefetch=1,
            grid=(S_DEV // step,),
            in_specs=[
                pl.BlockSpec((1, 1, 256, T_DEV), lambda i, index: (index[0], half, 0, 0)),
                pl.BlockSpec((step, HALF, T_DEV), lambda i, index: (i, chunk, 0)),
            ]
            + ([] if other is None else [by_d])
            + [pl.BlockSpec((8, 128), lambda i, index: (0, 0))] * len(places)
            + [ANY] * len(after),
            out_specs=out_specs,
        ),
        out_shape=out_shape,
        name=("other" if other is None else "mine") + ("_a", "_b")[chunk],
        **params(2 * 256 * 2048 * 1024, 7 << 20, 46),
    )(index, tables, traces, *([] if other is None else [other]), *places, *after)


def sum_a_body(own, yl, yh, both, *rest):
    out = rest[-1]
    out[:, 0] = own[...] + yh[...]
    out[:, 1] = yl[...] + both[...]


def sum_a(parts, after=()):
    return pl.pallas_call(
        sum_a_body,
        in_specs=[WHOLE] * N_Y + [ANY] * len(after),
        out_specs=WHOLE,
        out_shape=jax.ShapeDtypeStruct((N_XZ, 2, PAIRS, 8, 128), jnp.float32),
        name="sum_a",
        **params(1 << 18, 3 << 20),
    )(*parts, *after)


def split(value):
    high = value.astype(jnp.bfloat16)
    return high, (value - high.astype(jnp.float32)).astype(jnp.bfloat16)


def turn(index):
    index = index & (NT - 1)
    quadrant = (index + NT // 8) >> 10
    u = (index - (quadrant << 10)).astype(jnp.float32) * (2.0 * math.pi / NT)
    v = u * u
    sine = u + u * v * (-1.0 / 6 + v * (1.0 / 120 + v * (-1.0 / 5040 + v * (1.0 / 362880))))
    cosine = 1.0 + v * (-0.5 + v * (1.0 / 24 + v * (-1.0 / 720 + v * (1.0 / 40320 + v * (-1.0 / 3628800)))))
    odd = (quadrant & 1) == 1
    c = jnp.where(odd, sine, cosine)
    s = jnp.where(odd, cosine, sine)
    return jnp.where(((quadrant + 1) & 2) == 2, -c, c), jnp.where((quadrant & 2) == 2, -s, s)


def times(a, b):
    return a[0] * b[0] - a[1] * b[1], a[1] * b[0] + a[0] * b[1]


def phase_tables(n_d, base, yh, yl, slowness, positions, column, slow, high, low):
    slow[...] = jnp.broadcast_to(slowness[...].astype(jnp.float32), (NP, 128)).T.astype(jnp.int32)
    first = base[0] + yh[0] * 128 + yl[0] * 8
    rows = 16

    def step(i, _):
        row = pl.multiple_of(i * rows, rows)
        delay = (slow[pl.ds(row, rows), :] * positions) & (NT - 1)
        own = turn(first * delay)
        forms = [own]
        if n_d > 1:
            by_yl = turn((8 - 16 * yl[0]) * delay)
            by_yh = turn((128 - 256 * yh[0]) * delay)
            other = times(own, by_yh)
            forms = [own, times(own, by_yl), other, times(other, by_yl)]
        by_zh = turn(2 * delay)
        for d, value in enumerate(forms):
            for j in range(N_ZH):
                if j > 0:
                    value = times(value, by_zh)
                for k in range(2):
                    where = (d * N_ZH + j, pl.ds(k * NP + row, rows), slice(column, column + 128))
                    high[where], low[where] = split(value[k])
        return 0

    lax.fori_loop(0, NP // rows, step, 0)


def stack(high, low, real, imag):
    left = lax.broadcasted_iota(jnp.int32, real.shape, 1) < HALF
    even = jnp.where(left, real, pltpu.roll(imag, HALF, 1))
    odd = jnp.where(left, pltpu.roll(real, HALF, 1), imag)
    b_high, b_low = split(jnp.concatenate([even, odd], axis=0))
    both = jnp.dot(high, jnp.concatenate([b_high, b_low], axis=1), preferred_element_type=jnp.float32)
    res = both[:, :128] + (jnp.dot(low, b_high, preferred_element_type=jnp.float32) + both[:, 128:])
    cross = pltpu.roll(res[NP:], HALF, 1)
    left = lax.broadcasted_iota(jnp.int32, (NP, 128), 1) < HALF
    return res[:NP] + jnp.where(left, cross, -cross)


def slant_a_body(n_after, zh, base, yh, yl, slowness, places, data, *rest):
    outs, (slow, high, low) = rest[n_after : n_after + N_ZH], rest[n_after + N_ZH :]
    for parity in range(2):
        for place in range(2):
            row = 2 * place + parity
            positions = places[row : row + 1, :].astype(jnp.int32)
            phase_tables(1, base, yh, yl, slowness, positions, (2 * parity + place) * 128, slow, high, low)
    for e, out in enumerate(outs):
        j = (zh[0] + e) & (N_ZH - 1)
        cols = []
        for part in range(2):
            rows = [data[:, pl.ds(place * PAIRS * 8 + 2 * j + part, PAIRS, stride=8), :] for place in range(2)]
            cols.append(jnp.concatenate([row.reshape(N_XZ * PAIRS, 128) for row in rows], axis=0))
        out[...] = stack(high[j], low[j], *cols)


def slant_a(zh, base, yh, yl, slowness, places, data, after=()):
    return pl.pallas_call(
        functools.partial(slant_a_body, len(after)),
        in_specs=[SCALAR] * 4 + [WHOLE] * 3 + [ANY] * len(after),
        out_specs=[WHOLE] * N_ZH,
        out_shape=[jax.ShapeDtypeStruct((NP, 128), jnp.float32)] * N_ZH,
        scratch_shapes=[pltpu.VMEM((NP, 128), jnp.int32)] + [pltpu.VMEM((N_ZH, 2 * NP, 512), jnp.bfloat16)] * 2,
        name="slant_a",
        **params(1 << 30, 5 << 20),
    )(zh, base, yh, yl, slowness, places, data.reshape(N_XZ, 2 * PAIRS * 8, 128), *after)


def slant_b_body(n_after, base, yh, yl, slowness, data, *rest):
    rest = rest[n_after:]
    outs, here, (slow, high, low) = rest[:N_Y], rest[N_Y], rest[N_Y + 1 :]
    here[...] = jnp.sum(data[:, N_Y * PAIRS * 8 :, :], axis=0)
    for parity in range(2):
        row = here[parity : parity + 1, :].astype(jnp.int32)
        phase_tables(N_Y, base, yh, yl, slowness, row, parity * 128, slow, high, low)
    for d, out in enumerate(outs):
        for j in range(N_ZH):
            cols = [
                data[:, pl.ds(d * PAIRS * 8 + 2 * j + part, PAIRS, stride=8), :].reshape(N_XZ * PAIRS, 128)
                for part in range(2)
            ]
            out[j] = stack(high[d * N_ZH + j], low[d * N_ZH + j], *cols)


def slant_b(base, yh, yl, slowness, data, after=()):
    return pl.pallas_call(
        functools.partial(slant_b_body, len(after)),
        in_specs=[SCALAR] * 3 + [WHOLE] * 2 + [ANY] * len(after),
        out_specs=[WHOLE] * (N_Y + 1),
        out_shape=[jax.ShapeDtypeStruct((N_ZH, NP, 128), jnp.float32)] * N_Y + [jax.ShapeDtypeStruct((8, 128), jnp.float32)],
        scratch_shapes=[pltpu.VMEM((NP, 128), jnp.int32)] + [pltpu.VMEM((N_Y * N_ZH, 2 * NP, 256), jnp.bfloat16)] * 2,
        name="slant_b",
        **params(1 << 31, 7 << 20),
    )(base, yh, yl, slowness, data.reshape(N_XZ, (N_Y * PAIRS + 1) * 8, 128), *after)


def sum_b_body(zh, own, yl, yh, both, *rest):
    outs = rest[-N_ZH:]
    for e, out in enumerate(outs):
        j = (zh[0] + e) & (N_ZH - 1)
        out[...] = (own[j] + yl[j]) + (yh[j] + both[j])


def sum_b(zh, parts, after=()):
    return pl.pallas_call(
        sum_b_body,
        in_specs=[SCALAR] + [WHOLE] * N_Y + [ANY] * len(after),
        out_specs=[WHOLE] * N_ZH,
        out_shape=[jax.ShapeDtypeStruct((NP, 128), jnp.float32)] * N_ZH,
        name="sum_b",
        **params(1 << 18, 1 << 20),
    )(zh, *parts, *after)


def finish_body(*refs):
    scale = jnp.float32(1.0 / math.sqrt(NT) / math.sqrt(SHOTS))
    left = lax.broadcasted_iota(jnp.int32, (NP, 128), 1) < HALF
    total = lambda four: ((four[0][...] + four[1][...]) + (four[2][...] + four[3][...])) * scale
    a, b, out = total(refs[:4]), total(refs[4:8]), refs[8]
    out[0, 0] = jnp.where(left, a, pltpu.roll(b, HALF, 1))
    out[0, 1] = jnp.where(left, pltpu.roll(a, HALF, 1), b)


def finish(parts):
    return pl.pallas_call(
        finish_body,
        in_specs=[WHOLE] * 8,
        out_specs=WHOLE,
        out_shape=jax.ShapeDtypeStruct((1, 2, NP, REC), jnp.float32),
        name="finish",
        **params(1 << 18, 1 << 20),
    )(*parts)


def swap(value, axes, size, mask):
    return lax.ppermute(value, axes, [(i, i ^ mask) for i in range(size)])


def exchange_y(parts):
    return [parts[0]] + [swap(parts[d], ("yh", "yl"), N_Y, d) for d in range(1, N_Y)]


def exchange_z(parts):
    shift = lambda e: [(i, (i + e) % N_ZH) for i in range(N_ZH)]
    return [parts[0]] + [lax.ppermute(parts[e], "zh", shift(e)) for e in range(1, N_ZH)]


def body(traces, shot_pos, slowness):
    yh, c, x, yl, zh, zl = (lax.axis_index(name) for name in FINE)
    one = lambda value: value.reshape(1)

    slot = (jnp.arange(N_XZ) == x * 2 + zl).astype(jnp.int32)
    places = (shot_pos.reshape(1, PAIRS, 2) * slot[:, None, None]).reshape(N_XZ * PAIRS, 2).T
    places = jnp.pad(places.astype(jnp.float32), ((0, 6), (0, 0)))

    tables = jnp.asarray(dft_tables())
    index = one(yh * 4 + c * 2 + yl)
    other_a = dft(index, tables, traces, 1, 0)
    other_b = dft(index, tables, traces, 1, 1, after=[other_a])
    mine_a = dft(index, tables, traces, 0, 0, swap(other_a, "c", 2, 1), after=[other_b])
    there = swap(places, "yl", 2, 1)
    mine_b = dft(index, tables, traces, 0, 1, swap(other_b, "c", 2, 1), after=[mine_a[0]], places=[places, there])
    data_b = lax.all_to_all(mine_b, ("x", "zl"), 0, 0, tiled=True)
    both_a = sum_a(exchange_y(mine_a), after=[mine_b])
    data_a = lax.all_to_all(both_a, ("x", "zl"), 0, 0, tiled=True)

    where = one(FREQ0 + c * 64 + x * 16 + zl), one(yh), one(yl), slowness.reshape(1, NP)
    *part_b, places = slant_b(*where, data_b, after=[both_a])
    part_b = exchange_y(part_b)
    part_a = slant_a(one(zh), *where, places, data_a)
    part_b = sum_b(one(zh), part_b, after=[part_a[0]])
    return finish([*exchange_z(part_a), *exchange_z(part_b)])


def solution(mesh):
    fine = Mesh(mesh.devices.reshape(SIZES), FINE)
    shot, tm = ("x", "yl", "zh", "zl"), ("yh", "c")
    return jax.shard_map(
        body,
        mesh=fine,
        in_specs=(P(shot, None, tm), P(shot), P()),
        out_specs=P(tm + shot, None, None, None),
        check_vma=False,
    )
```

```python
import functools
import math

import jax
import jax.numpy as jnp
import numpy as np
from jax import lax
from jax.experimental import pallas as pl
from jax.experimental.pallas import tpu as pltpu
from jax.sharding import Mesh, PartitionSpec as P

NT = 4096
REC = 128
NP = 128
FREQ0 = 16
S_DEV = 32
T_DEV = 1024
SHOTS = 2048
HALF = REC // 2
PAIRS = S_DEV // 2
FINE = ("yh", "c", "x", "yl", "zh", "zl")
SIZES = (2, 2, 4, 2, 4, 2)
N_Y = 4
N_XZ = 8
N_ZH = 4
MIB = 1024 * 1024
WHOLE = pl.BlockSpec(memory_space=pltpu.VMEM)
SCALAR = pl.BlockSpec(memory_space=pltpu.SMEM)
ANY = pl.BlockSpec(memory_space=pl.ANY)


def params(flops, size, vmem=24):
    return dict(
        compiler_params=pltpu.CompilerParams(vmem_limit_bytes=vmem * MIB),
        cost_estimate=pl.CostEstimate(flops=flops, bytes_accessed=size, transcendentals=0),
    )


def dft_tables():
    d, x, zl, zh = np.meshgrid(*(np.arange(n) for n in (N_Y, 4, 2, N_ZH)), indexing="ij")
    out = np.empty((2, 2, 2, 2, 128, 2, T_DEV), np.float64)
    for yh, c, yl, half in np.ndindex(2, 2, 2, 2):
        t = (yh * 2 + c) * T_DEV + np.arange(T_DEV)
        f = (yh ^ (d >> 1)) * 128 + (c ^ half) * 64 + x * 16 + (yl ^ (d & 1)) * 8 + zh * 2 + zl
        angle = ((FREQ0 + f).reshape(-1, 1) * t % NT) * (2.0 * math.pi / NT)
        out[yh, c, yl, half, :, 0] = np.cos(angle)
        out[yh, c, yl, half, :, 1] = -np.sin(angle)
    return out.reshape(8, 2, 256, T_DEV).astype(np.float32).astype(jnp.bfloat16)


def spectra(table, traces):
    rows = traces.shape[0]
    res = lax.dot_general(
        table[0, 0], traces[...].reshape(rows * HALF, T_DEV), (((1,), (1,)), ((), ())), preferred_element_type=jnp.float32
    )
    return [res[:, s * 128 : (s + 1) * 128].reshape(N_Y, N_XZ, 8, 128) for s in range(rows // 2)]


def other_body(n_after, index, table, traces, *rest):
    out = rest[n_after]
    for s, block in enumerate(spectra(table, traces)):
        out[:, :, s] = block


def mine_a_body(n_after, index, table, traces, other, *rest):
    outs = rest[n_after:]
    for s, block in enumerate(spectra(table, traces)):
        for d, out in enumerate(outs):
            out[:, s] = block[d] + other[d, :, s]


def mine_b_body(n_after, index, table, traces, other, here, there, *rest):
    out = rest[n_after]
    step = pl.program_id(0)
    blocks = spectra(table, traces)
    for s, block in enumerate(blocks):
        for d in range(N_Y):
            out[:, d * PAIRS + step * len(blocks) + s] = block[d] + other[d, :, s]

    @pl.when(step == 0)
    def _():
        tile = jnp.concatenate([here[:2], there[:2], jnp.zeros((4, 128), jnp.float32)], axis=0)
        out[:, N_Y * PAIRS] = jnp.broadcast_to(tile, (N_XZ, 8, 128))


def dft(index, tables, traces, half, chunk, other=None, after=(), places=()):
    step = 16
    n = step // 2
    by_d = pl.BlockSpec((N_Y, N_XZ, n, 8, 128), lambda i, index: (0, 0, i, 0, 0))
    f32 = lambda *shape: jax.ShapeDtypeStruct(shape, jnp.float32)
    if other is None:
        body, out_specs, out_shape = other_body, by_d, f32(N_Y, N_XZ, PAIRS, 8, 128)
    elif chunk == 0:
        body = mine_a_body
        out_specs = [pl.BlockSpec((N_XZ, n, 8, 128), lambda i, index: (0, i, 0, 0))] * N_Y
        out_shape = [f32(N_XZ, PAIRS, 8, 128)] * N_Y
    else:
        body = mine_b_body
        out_specs = pl.BlockSpec((N_XZ, N_Y * PAIRS + 1, 8, 128), lambda i, index: (0, 0, 0, 0))
        out_shape = f32(N_XZ, N_Y * PAIRS + 1, 8, 128)
    return pl.pallas_call(
        functools.partial(body, len(after)),
        grid_spec=pltpu.PrefetchScalarGridSpec(
            num_scalar_prefetch=1,
            grid=(S_DEV // step,),
            in_specs=[
                pl.BlockSpec((1, 1, 256, T_DEV), lambda i, index: (index[0], half, 0, 0)),
                pl.BlockSpec((step, HALF, T_DEV), lambda i, index: (i, chunk, 0)),
            ]
            + ([] if other is None else [by_d])
            + [pl.BlockSpec((8, 128), lambda i, index: (0, 0))] * len(places)
            + [ANY] * len(after),
            out_specs=out_specs,
        ),
        out_shape=out_shape,
        name=("other" if other is None else "mine") + ("_a", "_b")[chunk],
        **params(2 * 256 * 2048 * 1024, 7 << 20, 44),
    )(index, tables, traces, *([] if other is None else [other]), *places, *after)


def sum_a_body(own, yl, yh, both, *rest):
    out = rest[-1]
    out[:, 0] = own[...] + yh[...]
    out[:, 1] = yl[...] + both[...]


def sum_a(parts, after=()):
    return pl.pallas_call(
        sum_a_body,
        in_specs=[WHOLE] * N_Y + [ANY] * len(after),
        out_specs=WHOLE,
        out_shape=jax.ShapeDtypeStruct((N_XZ, 2, PAIRS, 8, 128), jnp.float32),
        name="sum_a",
        **params(1 << 18, 3 << 20),
    )(*parts, *after)


def split(value):
    high = value.astype(jnp.bfloat16)
    return high, (value - high.astype(jnp.float32)).astype(jnp.bfloat16)


def turn(index):
    index = index & (NT - 1)
    quadrant = (index + NT // 8) >> 10
    u = (index - (quadrant << 10)).astype(jnp.float32) * (2.0 * math.pi / NT)
    v = u * u
    sine = u + u * v * (-1.0 / 6 + v * (1.0 / 120 + v * (-1.0 / 5040 + v * (1.0 / 362880))))
    cosine = 1.0 + v * (-0.5 + v * (1.0 / 24 + v * (-1.0 / 720 + v * (1.0 / 40320 + v * (-1.0 / 3628800)))))
    odd = (quadrant & 1) == 1
    c = jnp.where(odd, sine, cosine)
    s = jnp.where(odd, cosine, sine)
    return jnp.where(((quadrant + 1) & 2) == 2, -c, c), jnp.where((quadrant & 2) == 2, -s, s)


def times(a, b):
    return a[0] * b[0] - a[1] * b[1], a[1] * b[0] + a[0] * b[1]


def phase_tables(n_d, base, yh, yl, slowness, positions, column, slow, high, low):
    slow[...] = jnp.broadcast_to(slowness[...].astype(jnp.float32), (NP, 128)).T.astype(jnp.int32)
    first = base[0] + yh[0] * 128 + yl[0] * 8
    rows = 32

    def step(i, _):
        row = pl.multiple_of(i * rows, rows)
        delay = (slow[pl.ds(row, rows), :] * positions) & (NT - 1)
        own, by_zh = turn(first * delay), turn(2 * delay)
        forms = [own]
        if n_d > 1:
            by_4 = times(by_zh, by_zh)
            by_8 = times(by_4, by_4)
            by_yl = by_8[0], jnp.where(yl[0] == 0, by_8[1], -by_8[1])
            by_yh = turn((128 - 256 * yh[0]) * delay)
            other = times(own, by_yh)
            forms = [own, times(own, by_yl), other, times(other, by_yl)]
        for d, value in enumerate(forms):
            for j in range(N_ZH):
                if j > 0:
                    value = times(value, by_zh)
                for k in range(2):
                    where = (d * N_ZH + j, pl.ds(k * NP + row, rows), slice(column, column + 128))
                    high[where], low[where] = split(value[k])
        return 0

    lax.fori_loop(0, NP // rows, step, 0)


def stack(high, low, real, imag):
    left = lax.broadcasted_iota(jnp.int32, real.shape, 1) < HALF
    even = jnp.where(left, real, pltpu.roll(imag, HALF, 1))
    odd = jnp.where(left, pltpu.roll(real, HALF, 1), imag)
    b_high, b_low = split(jnp.concatenate([even, odd], axis=0))
    both = jnp.dot(high, jnp.concatenate([b_high, b_low], axis=1), preferred_element_type=jnp.float32)
    res = both[:, :128] + (jnp.dot(low, b_high, preferred_element_type=jnp.float32) + both[:, 128:])
    cross = pltpu.roll(res[NP:], HALF, 1)
    left = lax.broadcasted_iota(jnp.int32, (NP, 128), 1) < HALF
    return res[:NP] + jnp.where(left, cross, -cross)


def phase_a_body(base, yh, yl, slowness, places, high, low, slow):
    for parity in range(2):
        for place in range(2):
            row = 2 * place + parity
            positions = places[row : row + 1, :].astype(jnp.int32)
            phase_tables(1, base, yh, yl, slowness, positions, (2 * parity + place) * 128, slow, high, low)


def phase_a(base, yh, yl, slowness, places):
    return pl.pallas_call(
        phase_a_body,
        in_specs=[SCALAR] * 3 + [WHOLE] * 2,
        out_specs=[WHOLE] * 2,
        out_shape=[jax.ShapeDtypeStruct((N_ZH, 2 * NP, 512), jnp.bfloat16)] * 2,
        scratch_shapes=[pltpu.VMEM((NP, 128), jnp.int32)],
        name="phase_a",
        **params(1 << 24, 2 << 20),
    )(base, yh, yl, slowness, places)


def slant_a_body(zh, high, low, data, *outs):
    for e, out in enumerate(outs):
        j = (zh[0] + e) & (N_ZH - 1)
        cols = []
        for part in range(2):
            rows = [data[:, pl.ds(place * PAIRS * 8 + 2 * j + part, PAIRS, stride=8), :] for place in range(2)]
            cols.append(jnp.concatenate([row.reshape(N_XZ * PAIRS, 128) for row in rows], axis=0))
        out[...] = stack(high[j], low[j], *cols)


def slant_a(zh, high, low, data):
    return pl.pallas_call(
        slant_a_body,
        in_specs=[SCALAR] + [WHOLE] * 3,
        out_specs=[WHOLE] * N_ZH,
        out_shape=[jax.ShapeDtypeStruct((NP, 128), jnp.float32)] * N_ZH,
        name="slant_a",
        **params(1 << 30, 5 << 20),
    )(zh, high, low, data.reshape(N_XZ, 2 * PAIRS * 8, 128))


def slant_b_body(n_after, base, yh, yl, slowness, data, *rest):
    rest = rest[n_after:]
    outs, here, (slow, high, low) = rest[:N_Y], rest[N_Y], rest[N_Y + 1 :]
    here[...] = jnp.sum(data[:, N_Y * PAIRS * 8 :, :], axis=0)
    for parity in range(2):
        row = here[parity : parity + 1, :].astype(jnp.int32)
        phase_tables(N_Y, base, yh, yl, slowness, row, parity * 128, slow, high, low)
    for d, out in enumerate(outs):
        for j in range(N_ZH):
            cols = [
                data[:, pl.ds(d * PAIRS * 8 + 2 * j + part, PAIRS, stride=8), :].reshape(N_XZ * PAIRS, 128)
                for part in range(2)
            ]
            out[j] = stack(high[d * N_ZH + j], low[d * N_ZH + j], *cols)


def slant_b(base, yh, yl, slowness, data, after=()):
    return pl.pallas_call(
        functools.partial(slant_b_body, len(after)),
        in_specs=[SCALAR] * 3 + [WHOLE] * 2 + [ANY] * len(after),
        out_specs=[WHOLE] * (N_Y + 1),
        out_shape=[jax.ShapeDtypeStruct((N_ZH, NP, 128), jnp.float32)] * N_Y + [jax.ShapeDtypeStruct((8, 128), jnp.float32)],
        scratch_shapes=[pltpu.VMEM((NP, 128), jnp.int32)] + [pltpu.VMEM((N_Y * N_ZH, 2 * NP, 256), jnp.bfloat16)] * 2,
        name="slant_b",
        **params(1 << 31, 7 << 20),
    )(base, yh, yl, slowness, data.reshape(N_XZ, (N_Y * PAIRS + 1) * 8, 128), *after)


def sum_b_body(zh, own, yl, yh, both, *rest):
    outs = rest[-N_ZH:]
    for e, out in enumerate(outs):
        j = (zh[0] + e) & (N_ZH - 1)
        out[...] = (own[j] + yl[j]) + (yh[j] + both[j])


def sum_b(zh, parts, after=()):
    return pl.pallas_call(
        sum_b_body,
        in_specs=[SCALAR] + [WHOLE] * N_Y + [ANY] * len(after),
        out_specs=[WHOLE] * N_ZH,
        out_shape=[jax.ShapeDtypeStruct((NP, 128), jnp.float32)] * N_ZH,
        name="sum_b",
        **params(1 << 18, 1 << 20),
    )(zh, *parts, *after)


def finish_body(*refs):
    scale = jnp.float32(1.0 / math.sqrt(NT) / math.sqrt(SHOTS))
    left = lax.broadcasted_iota(jnp.int32, (NP, 128), 1) < HALF
    total = lambda four: ((four[0][...] + four[1][...]) + (four[2][...] + four[3][...])) * scale
    a, b, out = total(refs[:4]), total(refs[4:8]), refs[8]
    out[0, 0] = jnp.where(left, a, pltpu.roll(b, HALF, 1))
    out[0, 1] = jnp.where(left, pltpu.roll(a, HALF, 1), b)


def finish(parts):
    return pl.pallas_call(
        finish_body,
        in_specs=[WHOLE] * 8,
        out_specs=WHOLE,
        out_shape=jax.ShapeDtypeStruct((1, 2, NP, REC), jnp.float32),
        name="finish",
        **params(1 << 18, 1 << 20),
    )(*parts)


def swap(value, axes, size, mask):
    return lax.ppermute(value, axes, [(i, i ^ mask) for i in range(size)])


def exchange_y(parts):
    return [parts[0]] + [swap(parts[d], ("yh", "yl"), N_Y, d) for d in range(1, N_Y)]


def exchange_z(parts):
    shift = lambda e: [(i, (i + e) % N_ZH) for i in range(N_ZH)]
    return [parts[0]] + [lax.ppermute(parts[e], "zh", shift(e)) for e in range(1, N_ZH)]


def body(traces, shot_pos, slowness):
    yh, c, x, yl, zh, zl = (lax.axis_index(name) for name in FINE)
    one = lambda value: value.reshape(1)

    slot = (jnp.arange(N_XZ) == x * 2 + zl).astype(jnp.int32)
    places = (shot_pos.reshape(1, PAIRS, 2) * slot[:, None, None]).reshape(N_XZ * PAIRS, 2).T
    places = jnp.pad(places.astype(jnp.float32), ((0, 6), (0, 0)))

    tables = jnp.asarray(dft_tables())
    index = one(yh * 4 + c * 2 + yl)
    other_a = dft(index, tables, traces, 1, 0)
    other_b = dft(index, tables, traces, 1, 1, after=[other_a])
    mine_a = dft(index, tables, traces, 0, 0, swap(other_a, "c", 2, 1), after=[other_b])
    there = swap(places, "yl", 2, 1)
    mine_b = dft(index, tables, traces, 0, 1, swap(other_b, "c", 2, 1), after=[mine_a[0]], places=[places, there])
    data_b = lax.all_to_all(mine_b, ("x", "zl"), 0, 0, tiled=True)
    both_a = sum_a(exchange_y(mine_a), after=[mine_b])
    data_a = lax.all_to_all(both_a, ("x", "zl"), 0, 0, tiled=True)

    where = one(FREQ0 + c * 64 + x * 16 + zl), one(yh), one(yl), slowness.reshape(1, NP)
    *part_b, places = slant_b(*where, data_b, after=[both_a])
    part_b = exchange_y(part_b)
    part_a = slant_a(one(zh), *phase_a(*where, places), data_a)
    part_b = sum_b(one(zh), part_b, after=[part_a[0]])
    return finish([*exchange_z(part_a), *exchange_z(part_b)])


def solution(mesh):
    fine = Mesh(mesh.devices.reshape(SIZES), FINE)
    shot, tm = ("x", "yl", "zh", "zl"), ("yh", "c")
    return jax.shard_map(
        body,
        mesh=fine,
        in_specs=(P(shot, None, tm), P(shot), P()),
        out_specs=P(tm + shot, None, None, None),
        check_vma=False,
    )
```

```python
import functools
import math

import jax
import jax.numpy as jnp
import numpy as np
from jax import lax
from jax.experimental import pallas as pl
from jax.experimental.pallas import tpu as pltpu
from jax.sharding import Mesh, PartitionSpec as P

NT = 4096
REC = 128
NP = 128
FREQ0 = 16
S_DEV = 32
T_DEV = 1024
SHOTS = 2048
HALF = REC // 2
PAIRS = S_DEV // 2
FINE = ("yh", "c", "x", "yl", "zh", "zl")
SIZES = (2, 2, 4, 2, 4, 2)
N_Y = 4
N_XZ = 8
N_ZH = 4
MIB = 1024 * 1024
WHOLE = pl.BlockSpec(memory_space=pltpu.VMEM)
SCALAR = pl.BlockSpec(memory_space=pltpu.SMEM)
ANY = pl.BlockSpec(memory_space=pl.ANY)


def params(flops, size, vmem=24):
    return dict(
        compiler_params=pltpu.CompilerParams(vmem_limit_bytes=vmem * MIB),
        cost_estimate=pl.CostEstimate(flops=flops, bytes_accessed=size, transcendentals=0),
    )


def dft_tables():
    d, x, zl, zh = np.meshgrid(*(np.arange(n) for n in (N_Y, 4, 2, N_ZH)), indexing="ij")
    out = np.empty((2, 2, 2, 2, 128, 2, T_DEV), np.float64)
    for yh, c, yl, half in np.ndindex(2, 2, 2, 2):
        t = (yh * 2 + c) * T_DEV + np.arange(T_DEV)
        f = (yh ^ (d >> 1)) * 128 + (c ^ half) * 64 + x * 16 + (yl ^ (d & 1)) * 8 + zh * 2 + zl
        angle = ((FREQ0 + f).reshape(-1, 1) * t % NT) * (2.0 * math.pi / NT)
        out[yh, c, yl, half, :, 0] = np.cos(angle)
        out[yh, c, yl, half, :, 1] = -np.sin(angle)
    return out.reshape(8, 2, 256, T_DEV).astype(np.float32).astype(jnp.bfloat16)


def spectra(table, traces):
    rows = traces.shape[0]
    res = lax.dot_general(
        table[0, 0], traces[...].reshape(rows * HALF, T_DEV), (((1,), (1,)), ((), ())), preferred_element_type=jnp.float32
    )
    return [res[:, s * 128 : (s + 1) * 128].reshape(N_Y, N_XZ, 8, 128) for s in range(rows // 2)]


def other_body(n_after, index, table, traces, *rest):
    out = rest[n_after]
    for s, block in enumerate(spectra(table, traces)):
        out[:, :, s] = block


def mine_a_body(n_after, index, table, traces, other, *rest):
    outs = rest[n_after:]
    for s, block in enumerate(spectra(table, traces)):
        for d, out in enumerate(outs):
            out[:, s] = block[d] + other[d, :, s]


def mine_b_body(n_after, index, table, traces, other, here, there, *rest):
    out = rest[n_after]
    step = pl.program_id(0)
    blocks = spectra(table, traces)
    for s, block in enumerate(blocks):
        for d in range(N_Y):
            out[:, d * PAIRS + step * len(blocks) + s] = block[d] + other[d, :, s]

    @pl.when(step == 0)
    def _():
        tile = jnp.concatenate([here[:2], there[:2], jnp.zeros((4, 128), jnp.float32)], axis=0)
        out[:, N_Y * PAIRS] = jnp.broadcast_to(tile, (N_XZ, 8, 128))


def dft(index, tables, traces, half, chunk, other=None, after=(), places=()):
    step = 16
    n = step // 2
    by_d = pl.BlockSpec((N_Y, N_XZ, n, 8, 128), lambda i, index: (0, 0, i, 0, 0))
    f32 = lambda *shape: jax.ShapeDtypeStruct(shape, jnp.float32)
    if other is None:
        body, out_specs, out_shape = other_body, by_d, f32(N_Y, N_XZ, PAIRS, 8, 128)
    elif chunk == 0:
        body = mine_a_body
        out_specs = [pl.BlockSpec((N_XZ, n, 8, 128), lambda i, index: (0, i, 0, 0))] * N_Y
        out_shape = [f32(N_XZ, PAIRS, 8, 128)] * N_Y
    else:
        body = mine_b_body
        out_specs = pl.BlockSpec((N_XZ, N_Y * PAIRS + 1, 8, 128), lambda i, index: (0, 0, 0, 0))
        out_shape = f32(N_XZ, N_Y * PAIRS + 1, 8, 128)
    return pl.pallas_call(
        functools.partial(body, len(after)),
        grid_spec=pltpu.PrefetchScalarGridSpec(
            num_scalar_prefetch=1,
            grid=(S_DEV // step,),
            in_specs=[
                pl.BlockSpec((1, 1, 256, T_DEV), lambda i, index: (index[0], half, 0, 0)),
                pl.BlockSpec((step, HALF, T_DEV), lambda i, index: (i, chunk, 0)),
            ]
            + ([] if other is None else [by_d])
            + [pl.BlockSpec((8, 128), lambda i, index: (0, 0))] * len(places)
            + [ANY] * len(after),
            out_specs=out_specs,
        ),
        out_shape=out_shape,
        name=("other" if other is None else "mine") + ("_a", "_b")[chunk],
        **params(2 * 256 * 2048 * 1024, 7 << 20, 44),
    )(index, tables, traces, *([] if other is None else [other]), *places, *after)


def sum_a_body(own, yl, yh, both, *rest):
    out = rest[-1]
    out[:, 0] = own[...] + yh[...]
    out[:, 1] = yl[...] + both[...]


def sum_a(parts, after=()):
    return pl.pallas_call(
        sum_a_body,
        in_specs=[WHOLE] * N_Y + [ANY] * len(after),
        out_specs=WHOLE,
        out_shape=jax.ShapeDtypeStruct((N_XZ, 2, PAIRS, 8, 128), jnp.float32),
        name="sum_a",
        **params(1 << 18, 3 << 20),
    )(*parts, *after)


def split(value):
    high = value.astype(jnp.bfloat16)
    return high, (value - high.astype(jnp.float32)).astype(jnp.bfloat16)


def turn(index):
    index = index & (NT - 1)
    quadrant = (index + NT // 8) >> 10
    u = (index - (quadrant << 10)).astype(jnp.float32) * (2.0 * math.pi / NT)
    v = u * u
    sine = u + u * v * (-1.0 / 6 + v * (1.0 / 120 + v * (-1.0 / 5040 + v * (1.0 / 362880))))
    cosine = 1.0 + v * (-0.5 + v * (1.0 / 24 + v * (-1.0 / 720 + v * (1.0 / 40320 + v * (-1.0 / 3628800)))))
    odd = (quadrant & 1) == 1
    c = jnp.where(odd, sine, cosine)
    s = jnp.where(odd, cosine, sine)
    return jnp.where(((quadrant + 1) & 2) == 2, -c, c), jnp.where((quadrant & 2) == 2, -s, s)


def times(a, b):
    return a[0] * b[0] - a[1] * b[1], a[1] * b[0] + a[0] * b[1]


def phase_tables(n_d, base, yh, yl, slowness, positions, column, slow, high, low):
    slow[...] = jnp.broadcast_to(slowness[...].astype(jnp.float32), (NP, 128)).T.astype(jnp.int32)
    first = base[0] + yh[0] * 128 + yl[0] * 8
    rows = 32

    def step(i, _):
        row = pl.multiple_of(i * rows, rows)
        delay = (slow[pl.ds(row, rows), :] * positions) & (NT - 1)
        own, by_zh = turn(first * delay), turn(2 * delay)
        forms = [own]
        if n_d > 1:
            by_4 = times(by_zh, by_zh)
            by_8 = times(by_4, by_4)
            by_yl = by_8[0], jnp.where(yl[0] == 0, by_8[1], -by_8[1])
            by_yh = turn((128 - 256 * yh[0]) * delay)
            other = times(own, by_yh)
            forms = [own, times(own, by_yl), other, times(other, by_yl)]
        for d, value in enumerate(forms):
            for j in range(N_ZH):
                if j > 0:
                    value = times(value, by_zh)
                for k in range(2):
                    where = (d * N_ZH + j, pl.ds(k * NP + row, rows), slice(column, column + 128))
                    high[where], low[where] = split(value[k])
        return 0

    lax.fori_loop(0, NP // rows, step, 0)


def stack(high, low, real, imag):
    left = lax.broadcasted_iota(jnp.int32, real.shape, 1) < HALF
    even = jnp.where(left, real, pltpu.roll(imag, HALF, 1))
    odd = jnp.where(left, pltpu.roll(real, HALF, 1), imag)
    b_high, b_low = split(jnp.concatenate([even, odd], axis=0))
    both = jnp.dot(high, jnp.concatenate([b_high, b_low], axis=1), preferred_element_type=jnp.float32)
    res = both[:, :128] + (jnp.dot(low, b_high, preferred_element_type=jnp.float32) + both[:, 128:])
    cross = pltpu.roll(res[NP:], HALF, 1)
    left = lax.broadcasted_iota(jnp.int32, (NP, 128), 1) < HALF
    return res[:NP] + jnp.where(left, cross, -cross)


def phase_a_body(base, yh, yl, slowness, places, high, low, slow):
    for parity in range(2):
        for place in range(2):
            row = 2 * place + parity
            positions = places[row : row + 1, :].astype(jnp.int32)
            phase_tables(1, base, yh, yl, slowness, positions, (2 * parity + place) * 128, slow, high, low)


def phase_a(base, yh, yl, slowness, places):
    return pl.pallas_call(
        phase_a_body,
        in_specs=[SCALAR] * 3 + [WHOLE] * 2,
        out_specs=[WHOLE] * 2,
        out_shape=[jax.ShapeDtypeStruct((N_ZH, 2 * NP, 512), jnp.bfloat16)] * 2,
        scratch_shapes=[pltpu.VMEM((NP, 128), jnp.int32)],
        name="phase_a",
        **params(1 << 24, 2 << 20),
    )(base, yh, yl, slowness, places)


def slant_a_body(zh, high, low, data, *outs):
    for e, out in enumerate(outs):
        j = (zh[0] + e) & (N_ZH - 1)
        cols = []
        for part in range(2):
            rows = [data[:, pl.ds(place * PAIRS * 8 + 2 * j + part, PAIRS, stride=8), :] for place in range(2)]
            cols.append(jnp.concatenate([row.reshape(N_XZ * PAIRS, 128) for row in rows], axis=0))
        out[...] = stack(high[j], low[j], *cols)


def slant_a(zh, high, low, data):
    return pl.pallas_call(
        slant_a_body,
        in_specs=[SCALAR] + [WHOLE] * 3,
        out_specs=[WHOLE] * N_ZH,
        out_shape=[jax.ShapeDtypeStruct((NP, 128), jnp.float32)] * N_ZH,
        name="slant_a",
        **params(1 << 30, 5 << 20),
    )(zh, high, low, data.reshape(N_XZ, 2 * PAIRS * 8, 128))


def slant_b_body(n_after, base, yh, yl, slowness, data, *rest):
    rest = rest[n_after:]
    outs, here, (slow, high, low) = rest[:N_Y], rest[N_Y], rest[N_Y + 1 :]
    here[...] = jnp.sum(data[:, N_Y * PAIRS * 8 :, :], axis=0)
    for parity in range(2):
        row = here[parity : parity + 1, :].astype(jnp.int32)
        phase_tables(N_Y, base, yh, yl, slowness, row, parity * 128, slow, high, low)
    for d, out in enumerate(outs):
        for j in range(N_ZH):
            cols = [
                data[:, pl.ds(d * PAIRS * 8 + 2 * j + part, PAIRS, stride=8), :].reshape(N_XZ * PAIRS, 128)
                for part in range(2)
            ]
            out[j] = stack(high[d * N_ZH + j], low[d * N_ZH + j], *cols)


def slant_b(base, yh, yl, slowness, data, after=()):
    return pl.pallas_call(
        functools.partial(slant_b_body, len(after)),
        in_specs=[SCALAR] * 3 + [WHOLE] * 2 + [ANY] * len(after),
        out_specs=[WHOLE] * (N_Y + 1),
        out_shape=[jax.ShapeDtypeStruct((N_ZH, NP, 128), jnp.float32)] * N_Y + [jax.ShapeDtypeStruct((8, 128), jnp.float32)],
        scratch_shapes=[pltpu.VMEM((NP, 128), jnp.int32)] + [pltpu.VMEM((N_Y * N_ZH, 2 * NP, 256), jnp.bfloat16)] * 2,
        name="slant_b",
        **params(1 << 31, 7 << 20),
    )(base, yh, yl, slowness, data.reshape(N_XZ, (N_Y * PAIRS + 1) * 8, 128), *after)


def sum_b_body(zh, own, yl, yh, both, *rest):
    halves, outs = rest[:N_ZH], rest[N_ZH:]
    for e, out in enumerate(outs):
        j = (zh[0] + e) & (N_ZH - 1)
        out[0] = halves[e][...]
        out[1] = (own[j] + yl[j]) + (yh[j] + both[j])


def sum_b(zh, parts, halves):
    return pl.pallas_call(
        sum_b_body,
        in_specs=[SCALAR] + [WHOLE] * (N_Y + N_ZH),
        out_specs=[WHOLE] * N_ZH,
        out_shape=[jax.ShapeDtypeStruct((2, NP, 128), jnp.float32)] * N_ZH,
        name="sum_b",
        **params(1 << 18, 1 << 20),
    )(zh, *parts, *halves)


def finish_body(own, *rest):
    scale = jnp.float32(1.0 / math.sqrt(NT) / math.sqrt(SHOTS))
    left = lax.broadcasted_iota(jnp.int32, (NP, 128), 1) < HALF
    out = rest[-1]
    a, b = (((own[i] + rest[0][i]) + (rest[1][i] + rest[2][i])) * scale for i in range(2))
    out[0, 0] = jnp.where(left, a, pltpu.roll(b, HALF, 1))
    out[0, 1] = jnp.where(left, pltpu.roll(a, HALF, 1), b)


def finish(parts):
    return pl.pallas_call(
        finish_body,
        in_specs=[WHOLE] * N_ZH,
        out_specs=WHOLE,
        out_shape=jax.ShapeDtypeStruct((1, 2, NP, REC), jnp.float32),
        name="finish",
        **params(1 << 18, 1 << 20),
    )(*parts)


def swap(value, axes, size, mask):
    return lax.ppermute(value, axes, [(i, i ^ mask) for i in range(size)])


def exchange_y(parts):
    return [parts[0]] + [swap(parts[d], ("yh", "yl"), N_Y, d) for d in range(1, N_Y)]


def exchange_z(parts):
    shift = lambda e: [(i, (i + e) % N_ZH) for i in range(N_ZH)]
    return [parts[0]] + [lax.ppermute(parts[e], "zh", shift(e)) for e in range(1, N_ZH)]


def body(traces, shot_pos, slowness):
    yh, c, x, yl, zh, zl = (lax.axis_index(name) for name in FINE)
    one = lambda value: value.reshape(1)

    slot = (jnp.arange(N_XZ) == x * 2 + zl).astype(jnp.int32)
    places = (shot_pos.reshape(1, PAIRS, 2) * slot[:, None, None]).reshape(N_XZ * PAIRS, 2).T
    places = jnp.pad(places.astype(jnp.float32), ((0, 6), (0, 0)))

    tables = jnp.asarray(dft_tables())
    index = one(yh * 4 + c * 2 + yl)
    other_a = dft(index, tables, traces, 1, 0)
    other_b = dft(index, tables, traces, 1, 1, after=[other_a])
    mine_a = dft(index, tables, traces, 0, 0, swap(other_a, "c", 2, 1), after=[other_b])
    there = swap(places, "yl", 2, 1)
    mine_b = dft(index, tables, traces, 0, 1, swap(other_b, "c", 2, 1), after=[mine_a[0]], places=[places, there])
    data_b = lax.all_to_all(mine_b, ("x", "zl"), 0, 0, tiled=True)
    both_a = sum_a(exchange_y(mine_a), after=[mine_b])
    data_a = lax.all_to_all(both_a, ("x", "zl"), 0, 0, tiled=True)

    where = one(FREQ0 + c * 64 + x * 16 + zl), one(yh), one(yl), slowness.reshape(1, NP)
    *part_b, places = slant_b(*where, data_b, after=[both_a])
    part_b = exchange_y(part_b)
    part_a = slant_a(one(zh), *phase_a(*where, places), data_a)
    return finish(exchange_z(sum_b(one(zh), part_b, part_a)))


def solution(mesh):
    fine = Mesh(mesh.devices.reshape(SIZES), FINE)
    shot, tm = ("x", "yl", "zh", "zl"), ("yh", "c")
    return jax.shard_map(
        body,
        mesh=fine,
        in_specs=(P(shot, None, tm), P(shot), P()),
        out_specs=P(tm + shot, None, None, None),
        check_vma=False,
    )
```

```python
import functools
import math

import jax
import jax.numpy as jnp
import numpy as np
from jax import lax
from jax.experimental import pallas as pl
from jax.experimental.pallas import tpu as pltpu
from jax.sharding import Mesh, PartitionSpec as P

NT = 4096
REC = 128
NP = 128
FREQ0 = 16
S_DEV = 32
T_DEV = 1024
SHOTS = 2048
HALF = REC // 2
PAIRS = S_DEV // 2
FINE = ("yh", "c", "x", "yl", "zh", "zl")
SIZES = (2, 2, 4, 2, 4, 2)
N_Y = 4
N_XZ = 8
N_ZH = 4
MIB = 1024 * 1024
WHOLE = pl.BlockSpec(memory_space=pltpu.VMEM)
SCALAR = pl.BlockSpec(memory_space=pltpu.SMEM)
ANY = pl.BlockSpec(memory_space=pl.ANY)


def params(flops, size, vmem=24):
    return dict(
        compiler_params=pltpu.CompilerParams(vmem_limit_bytes=vmem * MIB),
        cost_estimate=pl.CostEstimate(flops=flops, bytes_accessed=size, transcendentals=0),
    )


def dft_tables():
    d, x, zl, zh = np.meshgrid(*(np.arange(n) for n in (N_Y, 4, 2, N_ZH)), indexing="ij")
    out = np.empty((2, 2, 2, 2, 128, 2, T_DEV), np.float64)
    for yh, c, yl, half in np.ndindex(2, 2, 2, 2):
        t = (yh * 2 + c) * T_DEV + np.arange(T_DEV)
        f = (yh ^ (d >> 1)) * 128 + (c ^ half) * 64 + x * 16 + (yl ^ (d & 1)) * 8 + zh * 2 + zl
        angle = ((FREQ0 + f).reshape(-1, 1) * t % NT) * (2.0 * math.pi / NT)
        out[yh, c, yl, half, :, 0] = np.cos(angle)
        out[yh, c, yl, half, :, 1] = -np.sin(angle)
    return out.reshape(8, 2, 256, T_DEV).astype(np.float32).astype(jnp.bfloat16)


def spectra(table, traces):
    rows = traces.shape[0]
    res = lax.dot_general(
        table[0, 0], traces[...].reshape(rows * HALF, T_DEV), (((1,), (1,)), ((), ())), preferred_element_type=jnp.float32
    )
    return [res[:, s * 128 : (s + 1) * 128].reshape(N_Y, N_XZ, 8, 128) for s in range(rows // 2)]


def other_body(n_after, index, table, traces, *rest):
    out = rest[n_after]
    for s, block in enumerate(spectra(table, traces)):
        out[:, :, s] = block


def mine_a_body(n_after, index, table, traces, other, *rest):
    outs = rest[n_after:]
    for s, block in enumerate(spectra(table, traces)):
        for d, out in enumerate(outs):
            out[:, s] = block[d] + other[d, :, s]


def mine_b_body(n_after, index, table, traces, other, here, there, *rest):
    out = rest[n_after]
    step = pl.program_id(0)
    blocks = spectra(table, traces)
    for s, block in enumerate(blocks):
        for d in range(N_Y):
            out[:, d * PAIRS + step * len(blocks) + s] = block[d] + other[d, :, s]

    @pl.when(step == 0)
    def _():
        tile = jnp.concatenate([here[:2], there[:2], jnp.zeros((4, 128), jnp.float32)], axis=0)
        out[:, N_Y * PAIRS] = jnp.broadcast_to(tile, (N_XZ, 8, 128))


def dft(index, tables, traces, half, chunk, other=None, after=(), places=()):
    step = 16
    n = step // 2
    by_d = pl.BlockSpec((N_Y, N_XZ, n, 8, 128), lambda i, index: (0, 0, i, 0, 0))
    f32 = lambda *shape: jax.ShapeDtypeStruct(shape, jnp.float32)
    if other is None:
        body, out_specs, out_shape = other_body, by_d, f32(N_Y, N_XZ, PAIRS, 8, 128)
    elif chunk == 0:
        body = mine_a_body
        out_specs = [pl.BlockSpec((N_XZ, n, 8, 128), lambda i, index: (0, i, 0, 0))] * N_Y
        out_shape = [f32(N_XZ, PAIRS, 8, 128)] * N_Y
    else:
        body = mine_b_body
        out_specs = pl.BlockSpec((N_XZ, N_Y * PAIRS + 1, 8, 128), lambda i, index: (0, 0, 0, 0))
        out_shape = f32(N_XZ, N_Y * PAIRS + 1, 8, 128)
    return pl.pallas_call(
        functools.partial(body, len(after)),
        grid_spec=pltpu.PrefetchScalarGridSpec(
            num_scalar_prefetch=1,
            grid=(S_DEV // step,),
            in_specs=[
                pl.BlockSpec((1, 1, 256, T_DEV), lambda i, index: (index[0], half, 0, 0)),
                pl.BlockSpec((step, HALF, T_DEV), lambda i, index: (i, chunk, 0)),
            ]
            + ([] if other is None else [by_d])
            + [pl.BlockSpec((8, 128), lambda i, index: (0, 0))] * len(places)
            + [ANY] * len(after),
            out_specs=out_specs,
        ),
        out_shape=out_shape,
        name=("other" if other is None else "mine") + ("_a", "_b")[chunk],
        **params(2 * 256 * 2048 * 1024, 7 << 20, 44),
    )(index, tables, traces, *([] if other is None else [other]), *places, *after)


def sum_a_body(own, yl, yh, both, *rest):
    out = rest[-1]
    out[:, 0] = own[...] + yh[...]
    out[:, 1] = yl[...] + both[...]


def sum_a(parts, after=()):
    return pl.pallas_call(
        sum_a_body,
        in_specs=[WHOLE] * N_Y + [ANY] * len(after),
        out_specs=WHOLE,
        out_shape=jax.ShapeDtypeStruct((N_XZ, 2, PAIRS, 8, 128), jnp.float32),
        name="sum_a",
        **params(1 << 18, 3 << 20),
    )(*parts, *after)


def split(value):
    high = value.astype(jnp.bfloat16)
    return high, (value - high.astype(jnp.float32)).astype(jnp.bfloat16)


def turn(index):
    index = index & (NT - 1)
    quadrant = (index + NT // 8) >> 10
    u = (index - (quadrant << 10)).astype(jnp.float32) * (2.0 * math.pi / NT)
    v = u * u
    sine = u + u * v * (-1.0 / 6 + v * (1.0 / 120 + v * (-1.0 / 5040 + v * (1.0 / 362880))))
    cosine = 1.0 + v * (-0.5 + v * (1.0 / 24 + v * (-1.0 / 720 + v * (1.0 / 40320 + v * (-1.0 / 3628800)))))
    odd = (quadrant & 1) == 1
    c = jnp.where(odd, sine, cosine)
    s = jnp.where(odd, cosine, sine)
    return jnp.where(((quadrant + 1) & 2) == 2, -c, c), jnp.where((quadrant & 2) == 2, -s, s)


def times(a, b):
    return a[0] * b[0] - a[1] * b[1], a[1] * b[0] + a[0] * b[1]


def phase_tables(n_d, base, yh, yl, slowness, positions, column, slow, high, low):
    slow[...] = jnp.broadcast_to(slowness[...].astype(jnp.float32), (NP, 128)).T.astype(jnp.int32)
    first = base[0] + yh[0] * 128 + yl[0] * 8
    rows = 64

    def step(i, _):
        row = pl.multiple_of(i * rows, rows)
        delay = (slow[pl.ds(row, rows), :] * positions) & (NT - 1)
        own, by_zh = turn(first * delay), turn(2 * delay)
        forms = [own]
        if n_d > 1:
            by_4 = times(by_zh, by_zh)
            by_8 = times(by_4, by_4)
            by_yl = by_8[0], jnp.where(yl[0] == 0, by_8[1], -by_8[1])
            by_yh = turn((128 - 256 * yh[0]) * delay)
            other = times(own, by_yh)
            forms = [own, times(own, by_yl), other, times(other, by_yl)]
        for d, value in enumerate(forms):
            for j in range(N_ZH):
                if j > 0:
                    value = times(value, by_zh)
                for k in range(2):
                    where = (d * N_ZH + j, pl.ds(k * NP + row, rows), slice(column, column + 128))
                    high[where], low[where] = split(value[k])
        return 0

    lax.fori_loop(0, NP // rows, step, 0)


def stack(high, low, real, imag):
    left = lax.broadcasted_iota(jnp.int32, real.shape, 1) < HALF
    even = jnp.where(left, real, pltpu.roll(imag, HALF, 1))
    odd = jnp.where(left, pltpu.roll(real, HALF, 1), imag)
    b_high, b_low = split(jnp.concatenate([even, odd], axis=0))
    both = jnp.dot(high, jnp.concatenate([b_high, b_low], axis=1), preferred_element_type=jnp.float32)
    res = both[:, :128] + (jnp.dot(low, b_high, preferred_element_type=jnp.float32) + both[:, 128:])
    cross = pltpu.roll(res[NP:], HALF, 1)
    left = lax.broadcasted_iota(jnp.int32, (NP, 128), 1) < HALF
    return res[:NP] + jnp.where(left, cross, -cross)


def phase_a_body(base, yh, yl, slowness, places, high, low, slow):
    for parity in range(2):
        for place in range(2):
            row = 2 * place + parity
            positions = places[row : row + 1, :].astype(jnp.int32)
            phase_tables(1, base, yh, yl, slowness, positions, (2 * parity + place) * 128, slow, high, low)


def phase_a(base, yh, yl, slowness, places):
    return pl.pallas_call(
        phase_a_body,
        in_specs=[SCALAR] * 3 + [WHOLE] * 2,
        out_specs=[WHOLE] * 2,
        out_shape=[jax.ShapeDtypeStruct((N_ZH, 2 * NP, 512), jnp.bfloat16)] * 2,
        scratch_shapes=[pltpu.VMEM((NP, 128), jnp.int32)],
        name="phase_a",
        **params(1 << 24, 2 << 20),
    )(base, yh, yl, slowness, places)


def slant_a_body(zh, high, low, data, *outs):
    for e, out in enumerate(outs):
        j = (zh[0] + e) & (N_ZH - 1)
        cols = []
        for part in range(2):
            rows = [data[:, pl.ds(place * PAIRS * 8 + 2 * j + part, PAIRS, stride=8), :] for place in range(2)]
            cols.append(jnp.concatenate([row.reshape(N_XZ * PAIRS, 128) for row in rows], axis=0))
        out[...] = stack(high[j], low[j], *cols)


def slant_a(zh, high, low, data):
    return pl.pallas_call(
        slant_a_body,
        in_specs=[SCALAR] + [WHOLE] * 3,
        out_specs=[WHOLE] * N_ZH,
        out_shape=[jax.ShapeDtypeStruct((NP, 128), jnp.float32)] * N_ZH,
        name="slant_a",
        **params(1 << 30, 5 << 20),
    )(zh, high, low, data.reshape(N_XZ, 2 * PAIRS * 8, 128))


def slant_b_body(n_after, base, yh, yl, slowness, data, *rest):
    rest = rest[n_after:]
    outs, here, (slow, high, low) = rest[:N_Y], rest[N_Y], rest[N_Y + 1 :]
    here[...] = jnp.sum(data[:, N_Y * PAIRS * 8 :, :], axis=0)
    for parity in range(2):
        row = here[parity : parity + 1, :].astype(jnp.int32)
        phase_tables(N_Y, base, yh, yl, slowness, row, parity * 128, slow, high, low)
    for d, out in enumerate(outs):
        for j in range(N_ZH):
            cols = [
                data[:, pl.ds(d * PAIRS * 8 + 2 * j + part, PAIRS, stride=8), :].reshape(N_XZ * PAIRS, 128)
                for part in range(2)
            ]
            out[j] = stack(high[d * N_ZH + j], low[d * N_ZH + j], *cols)


def slant_b(base, yh, yl, slowness, data, after=()):
    return pl.pallas_call(
        functools.partial(slant_b_body, len(after)),
        in_specs=[SCALAR] * 3 + [WHOLE] * 2 + [ANY] * len(after),
        out_specs=[WHOLE] * (N_Y + 1),
        out_shape=[jax.ShapeDtypeStruct((N_ZH, NP, 128), jnp.float32)] * N_Y + [jax.ShapeDtypeStruct((8, 128), jnp.float32)],
        scratch_shapes=[pltpu.VMEM((NP, 128), jnp.int32)] + [pltpu.VMEM((N_Y * N_ZH, 2 * NP, 256), jnp.bfloat16)] * 2,
        name="slant_b",
        **params(1 << 31, 7 << 20),
    )(base, yh, yl, slowness, data.reshape(N_XZ, (N_Y * PAIRS + 1) * 8, 128), *after)


def sum_b_body(zh, own, yl, yh, both, *rest):
    halves, outs = rest[:N_ZH], rest[N_ZH:]
    for e, out in enumerate(outs):
        j = (zh[0] + e) & (N_ZH - 1)
        out[0] = halves[e][...]
        out[1] = (own[j] + yl[j]) + (yh[j] + both[j])


def sum_b(zh, parts, halves):
    return pl.pallas_call(
        sum_b_body,
        in_specs=[SCALAR] + [WHOLE] * (N_Y + N_ZH),
        out_specs=[WHOLE] * N_ZH,
        out_shape=[jax.ShapeDtypeStruct((2, NP, 128), jnp.float32)] * N_ZH,
        name="sum_b",
        **params(1 << 18, 1 << 20),
    )(zh, *parts, *halves)


def finish_body(own, *rest):
    scale = jnp.float32(1.0 / math.sqrt(NT) / math.sqrt(SHOTS))
    left = lax.broadcasted_iota(jnp.int32, (NP, 128), 1) < HALF
    out = rest[-1]
    a, b = (((own[i] + rest[0][i]) + (rest[1][i] + rest[2][i])) * scale for i in range(2))
    out[0, 0] = jnp.where(left, a, pltpu.roll(b, HALF, 1))
    out[0, 1] = jnp.where(left, pltpu.roll(a, HALF, 1), b)


def finish(parts):
    return pl.pallas_call(
        finish_body,
        in_specs=[WHOLE] * N_ZH,
        out_specs=WHOLE,
        out_shape=jax.ShapeDtypeStruct((1, 2, NP, REC), jnp.float32),
        name="finish",
        **params(1 << 18, 1 << 20),
    )(*parts)


def swap(value, axes, size, mask):
    return lax.ppermute(value, axes, [(i, i ^ mask) for i in range(size)])


def exchange_y(parts):
    return [parts[0]] + [swap(parts[d], ("yh", "yl"), N_Y, d) for d in range(1, N_Y)]


def exchange_z(parts):
    shift = lambda e: [(i, (i + e) % N_ZH) for i in range(N_ZH)]
    return [parts[0]] + [lax.ppermute(parts[e], "zh", shift(e)) for e in range(1, N_ZH)]


def body(traces, shot_pos, slowness):
    yh, c, x, yl, zh, zl = (lax.axis_index(name) for name in FINE)
    one = lambda value: value.reshape(1)

    slot = (jnp.arange(N_XZ) == x * 2 + zl).astype(jnp.int32)
    places = (shot_pos.reshape(1, PAIRS, 2) * slot[:, None, None]).reshape(N_XZ * PAIRS, 2).T
    places = jnp.pad(places.astype(jnp.float32), ((0, 6), (0, 0)))

    tables = jnp.asarray(dft_tables())
    index = one(yh * 4 + c * 2 + yl)
    other_a = dft(index, tables, traces, 1, 0)
    other_b = dft(index, tables, traces, 1, 1, after=[other_a])
    mine_a = dft(index, tables, traces, 0, 0, swap(other_a, "c", 2, 1), after=[other_b])
    there = swap(places, "yl", 2, 1)
    mine_b = dft(index, tables, traces, 0, 1, swap(other_b, "c", 2, 1), after=[mine_a[0]], places=[places, there])
    data_b = lax.all_to_all(mine_b, ("x", "zl"), 0, 0, tiled=True)
    both_a = sum_a(exchange_y(mine_a), after=[mine_b])
    data_a = lax.all_to_all(both_a, ("x", "zl"), 0, 0, tiled=True)

    where = one(FREQ0 + c * 64 + x * 16 + zl), one(yh), one(yl), slowness.reshape(1, NP)
    *part_b, places = slant_b(*where, data_b, after=[both_a])
    part_b = exchange_y(part_b)
    part_a = slant_a(one(zh), *phase_a(*where, places), data_a)
    return finish(exchange_z(sum_b(one(zh), part_b, part_a)))


def solution(mesh):
    fine = Mesh(mesh.devices.reshape(SIZES), FINE)
    shot, tm = ("x", "yl", "zh", "zl"), ("yh", "c")
    return jax.shard_map(
        body,
        mesh=fine,
        in_specs=(P(shot, None, tm), P(shot), P()),
        out_specs=P(tm + shot, None, None, None),
        check_vma=False,
    )
```
